32 devices in a mesh: dp: 4 (over z), row: 4 (over x, core), col: 2 (over y).
Axes of the slice: x: 2, y: 2, z: 4, core: 2. Of those that a mesh axis runs over, the one named last changes fastest.
Arguments:
- tokens: bfloat16 [32768, 1024], P(('dp', 'row'), 'col'), may hold values from -6 to 6
- ln1_gain: bfloat16 [1024], P('col'), may hold values from 0.25 to 1.75
- ln1_bias: bfloat16 [1024], P('col'), may hold values from -1.5 to 1.5
- qkv_weight: bfloat16 [1024, 3072], P('col', 'row'), may hold values from -0.1875 to 0.1875
- qkv_bias: bfloat16 [3072], P('row'), may hold values from -2.5 to 2.5
- out_weight: bfloat16 [1024, 1024], P('row', 'col'), may hold values from -0.5 to 0.5
- out_bias: bfloat16 [1024], P('col'), may hold values from -2.5 to 2.5
- ln2_gain: bfloat16 [1024], P('col'), may hold values from 0.25 to 1.75
- ln2_bias: bfloat16 [1024], P('col'), may hold values from -1.5 to 1.5
- up_weight: bfloat16 [1024, 4096], P('col', 'row'), may hold values from -0.1875 to 0.1875
- up_bias: bfloat16 [4096], P('row'), may hold values from -2.5 to 2.5
- down_weight: bfloat16 [4096, 1024], P('row', 'col'), may hold values from -0.09375 to 0.09375
- down_bias: bfloat16 [1024], P('col'), may hold values from -2.5 to 2.5
- cotangent: bfloat16 [32768, 1024], P(('dp', 'row'), 'col'), may hold values from -6 to 6
Outputs:
- output: float32 [32768, 1024], P(('dp', 'row'), 'col')
- input_grad: float32 [32768, 1024], P(('dp', 'row'), 'col')
- ln1_gain_grad: float32 [1024], P('col')
- ln1_bias_grad: float32 [1024], P('col')
- qkv_weight_grad: float32 [1024, 3072], P('col', 'row')
- qkv_bias_grad: float32 [3072], P('row')
- out_weight_grad: float32 [1024, 1024], P('row', 'col')
- out_bias_grad: float32 [1024], P('col')
- ln2_gain_grad: float32 [1024], P('col')
- ln2_bias_grad: float32 [1024], P('col')
- up_weight_grad: float32 [1024, 4096], P('col', 'row')
- up_bias_grad: float32 [4096], P('row')
- down_weight_grad: float32 [4096, 1024], P('row', 'col')
- down_bias_grad: float32 [1024], P('col')
The draws below stay inside these ranges and needn't reach their ends.
All inputs are finite; a program needn't handle non-finite values.
Results may differ from the reference program's by a relative error of at most 0.02.
Values may be sent and summed in bfloat16 or wider, within the bound.
A program may use at most 256 MiB of HBM per device.

```python
import math
import jax
import jax.numpy as jnp
from jax import lax

D = 1024
HEADS = 16
HEAD_DIM = 64
FF = 4096
SEQ_LEN = 1024
SEQ_GRP = 8
TOKENS = 32768
N_DP = 4


def block_scale(stream_key, shape, cuts, low, top_value):
    factor_of = 1.0
    for axis_at, blocks in cuts:
        heights = jax.random.uniform(jax.random.fold_in(jax.random.fold_in(stream_key, 6), axis_at), (blocks,), jnp.float32, low / len(cuts), top_value / len(cuts))
        factor_of = factor_of * jnp.repeat(jnp.exp(heights), shape[axis_at] // blocks).reshape((-1,) + (1,) * (len(shape) - 1 - axis_at))
    return factor_of


def normal_values(rng, extent, deviation, limit, split=(), kind=jnp.bfloat16):
    factor_of = block_scale(rng, extent, split, -0.22, 0.18) if split else 1.0
    values = jax.random.normal(rng, extent, jnp.float32) * deviation * factor_of
    return jnp.minimum(jnp.maximum(values, -limit), limit).astype(kind)


def setup_inputs(seed: int = 0) -> dict:
    arg_keys = jax.random.split(jax.random.key(seed), 15)
    tokens = normal_values(arg_keys[0], (TOKENS, D), 1.0, 6.0, ((0, 16), (1, 2)))
    ln1_gain = jnp.clip(1.0 + 0.15 * jax.random.normal(arg_keys[1], (D,), jnp.float32), 0.25, 1.75).astype(jnp.bfloat16)
    ln1_bias = normal_values(arg_keys[2], (D,), 0.3, 1.5, ((0, 2),))
    qkv_weight = normal_values(arg_keys[3], (D, 3 * D), D ** -0.5, 0.1875, ((0, 2), (1, 4)))
    qkv_bias = normal_values(arg_keys[4], (3 * D,), 0.5, 2.5, ((0, 4),))
    out_weight = normal_values(arg_keys[5], (D, D), (D // 8) ** -0.5, 0.5, ((0, 4), (1, 2)))
    out_bias = normal_values(arg_keys[6], (D,), 0.5, 2.5, ((0, 2),))
    ln2_gain = jnp.clip(1.0 + 0.15 * jax.random.normal(arg_keys[7], (D,), jnp.float32), 0.25, 1.75).astype(jnp.bfloat16)
    ln2_bias = normal_values(arg_keys[8], (D,), 0.3, 1.5, ((0, 2),))
    up_weight = normal_values(arg_keys[9], (D, FF), D ** -0.5, 0.1875, ((0, 2), (1, 4)))
    up_bias = normal_values(arg_keys[10], (FF,), 0.5, 2.5, ((0, 4),))
    down_weight = normal_values(arg_keys[11], (FF, D), FF ** -0.5, 0.09375, ((0, 4), (1, 2)))
    down_bias = normal_values(arg_keys[12], (D,), 0.5, 2.5, ((0, 2),))
    cotangent = normal_values(arg_keys[13], (TOKENS, D), 1.0, 6.0, ((0, 16), (1, 2)))
    return dict(tokens=tokens, ln1_gain=ln1_gain, ln1_bias=ln1_bias, qkv_weight=qkv_weight, qkv_bias=qkv_bias, out_weight=out_weight, out_bias=out_bias, ln2_gain=ln2_gain, ln2_bias=ln2_bias, up_weight=up_weight, up_bias=up_bias, down_weight=down_weight, down_bias=down_bias, cotangent=cotangent)


@jax.custom_vjp
def low(v):
    return lax.optimization_barrier(v.astype(jnp.bfloat16)).astype(jnp.float32)

@jax.custom_vjp
def low_back(v):
    return v

def low_keep(v):
    return (low(v), None)

def low_pass(kept, grad):
    return (grad,)

def back_keep(v):
    return (v, None)

def back_low(kept, grad):
    return (low(grad),)
low.defvjp(low_keep, low_pass)
low_back.defvjp(back_keep, back_low)
epsilon = 1e-05
highest = lax.Precision.HIGHEST

def bloom_gelu(values):
    return 0.5 * values * (1.0 + jnp.tanh(0.79788456 * values * (1.0 + 0.044715 * values * values)))

def layer_norm(rows, gain, shift):
    mean = lax.optimization_barrier(jnp.mean(rows, axis=-1, keepdims=True))
    centred = rows - mean
    spread = lax.optimization_barrier(jnp.mean(centred * centred, axis=-1, keepdims=True))
    return centred * lax.rsqrt(spread + epsilon) * gain + shift

def project(left, right):
    return jnp.einsum('nld,de->nle', left, right, precision=highest)

def forward(inputs, ln1_gain, ln1_bias, qkv_weight, qkv_bias, out_weight, out_bias, ln2_gain, ln2_bias, up_weight, up_bias, down_weight, down_bias):
    number = inputs.shape[0]
    normed_one = low(layer_norm(inputs, ln1_gain, ln1_bias))
    packed = low(low_back(project(normed_one, qkv_weight) + qkv_bias))
    packed = packed.reshape(number, SEQ_LEN, HEADS, 3, HEAD_DIM)
    queries = packed[:, :, :, 0]
    keys = packed[:, :, :, 1]
    values = packed[:, :, :, 2]
    position = jnp.arange(SEQ_LEN, dtype=jnp.int32)
    offset = position[None, :] - position[:, None]
    slopes = jnp.exp2(-8.0 * (jnp.arange(HEADS, dtype=jnp.float32) + 1.0) / HEADS)
    scores = jnp.einsum('nqhe,nkhe->nhqk', queries, keys, precision=highest) * (1.0 / math.sqrt(HEAD_DIM))
    scores = scores + slopes[:, None, None] * offset.astype(jnp.float32)[None]
    scores = low_back(jnp.where((offset <= 0)[None, None], scores, -1e+30))
    peak = lax.optimization_barrier(jnp.max(scores, axis=-1, keepdims=True))
    expo = jnp.exp(scores - peak)
    probs = low(expo / lax.optimization_barrier(jnp.sum(expo, axis=-1, keepdims=True)))
    context = jnp.einsum('nhqk,nkhe->nqhe', probs, values, precision=highest)
    context = low(low_back(context)).reshape(number, SEQ_LEN, D)
    resid = inputs + low_back(project(context, out_weight)) + out_bias
    normed_two = low(layer_norm(resid, ln2_gain, ln2_bias))
    upper = low_back(project(normed_two, up_weight) + up_bias)
    acts = low(bloom_gelu(upper))
    return resid + low_back(project(acts, down_weight)) + down_bias

def reference(tokens, ln1_gain, ln1_bias, qkv_weight, qkv_bias, out_weight, out_bias, ln2_gain, ln2_bias, up_weight, up_bias, down_weight, down_bias, cotangent):
    params = tuple((item.astype(jnp.float32) for item in (ln1_gain, ln1_bias, qkv_weight, qkv_bias, out_weight, out_bias, ln2_gain, ln2_bias, up_weight, up_bias, down_weight, down_bias)))
    total_seqs = SEQ_GRP * N_DP
    batch = math.gcd(total_seqs, max(1, 2048 // SEQ_LEN))
    rounds = total_seqs // batch
    inputs = tokens.astype(jnp.float32).reshape(rounds, batch, SEQ_LEN, D)
    grads_in = cotangent.astype(jnp.float32).reshape(rounds, batch, SEQ_LEN, D)

    def one_round(carry, pair):
        block_in, block_grad = pair
        result, pull = jax.vjp(forward, block_in, *params)
        pulled = pull(block_grad)
        carry = tuple((older + newer for older, newer in zip(carry, pulled[1:])))
        return (carry, (result, pulled[0]))
    zeros = tuple((jnp.zeros(item.shape, jnp.float32) for item in params))
    totals, (results, input_grads) = lax.scan(one_round, zeros, (inputs, grads_in))
    return (results.reshape(TOKENS, D), input_grads.reshape(TOKENS, D), totals[0], totals[1], totals[2], totals[3], totals[4], totals[5], totals[6], totals[7], totals[8], totals[9], totals[10], totals[11])
```

```python
import functools
import math

import jax
import jax.numpy as jnp
from jax import lax
from jax.experimental import pallas as pl
from jax.experimental.pallas import tpu as pltpu
from jax.sharding import PartitionSpec as P

D = 1024
HEADS = 16
HEAD_DIM = 64
SEQ_LEN = 1024


epsilon = 1e-05
masked = -1e30


def bloom_gelu(values):
    return 0.5 * values * (1.0 + jnp.tanh(0.79788456 * values * (1.0 + 0.044715 * values * values)))


def norm_forward(rows, gain, shift):
    middle = lax.psum(jnp.sum(rows, axis=1), "col") / D
    centred = rows - middle[:, None]
    spread = lax.psum(jnp.sum(centred * centred, axis=1), "col") / D
    inverse = lax.rsqrt(spread + epsilon)
    normed = centred * inverse[:, None]
    return (normed, inverse, (normed * gain + shift).astype(jnp.bfloat16))


def norm_backward(grad_rows, normed, inverse, gain):
    scaled = grad_rows * gain
    first, second = lax.psum((jnp.sum(scaled, axis=1), jnp.sum(scaled * normed, axis=1)), "col")
    return inverse[:, None] * (scaled - first[:, None] / D - normed * (second[:, None] / D))


def gather_rows(values):
    return lax.all_gather(values, "row", axis=0, tiled=True)


def gather_cols(values, backward):
    if backward:
        return lax.all_gather(values, "col", axis=0, tiled=True)
    return lax.all_gather(values, "col", axis=0, tiled=True)


def contract_whole(left, right, backward):
    contract = 1 if backward else 0
    return lax.dot_general(
        left, right, (((1,), (contract,)), ((), ())), preferred_element_type=jnp.float32
    )


def sum_cols(left, wide_right, backward):
    swapped = lax.all_to_all(left, "col", split_axis=0, concat_axis=1, tiled=True)
    return contract_whole(swapped, wide_right, backward)


def sum_rows(left, wide_right, backward):
    swapped = lax.all_to_all(left, "row", split_axis=0, concat_axis=1, tiled=True)
    return contract_whole(swapped, wide_right, backward)


def weight_grad(left, grad):
    return lax.dot_general(left, grad, (((0,), (0,)), ((), ())), preferred_element_type=jnp.float32)


def score_block(query_blk, keys, start, slopes):
    scores = jnp.einsum("qhe,khe->hqk", query_blk, keys, preferred_element_type=jnp.float32) * (
        1.0 / math.sqrt(HEAD_DIM)
    )
    shape = (query_blk.shape[0], keys.shape[0])
    offset = (
        lax.broadcasted_iota(jnp.int32, shape, 1)
        - lax.broadcasted_iota(jnp.int32, shape, 0)
        - start
    )
    scores = scores + slopes[:, None, None] * offset.astype(jnp.float32)[None]
    return jnp.where(offset[None] <= 0, scores, masked)


def split_heads(packed):
    heads_here = packed.shape[1] // (3 * HEAD_DIM)
    parted = packed.reshape(packed.shape[0] // SEQ_LEN, SEQ_LEN, heads_here, 3, HEAD_DIM)
    return (parted[:, :, :, 0], parted[:, :, :, 1], parted[:, :, :, 2])


def attention_forward(packed, slopes):
    queries, keys, values = split_heads(packed)
    length = min(512, SEQ_LEN)

    def one_sequence(triple):
        query_seq, key_seq, value_seq = triple

        def one_block(number):
            start = number * length
            query_blk = lax.dynamic_slice_in_dim(query_seq, start, length, 0)
            scores = score_block(query_blk, key_seq, start, slopes)
            highest = jnp.max(scores, axis=2, keepdims=True)
            expo = jnp.exp(scores - highest)
            totals = jnp.sum(expo, axis=2, keepdims=True)
            weights = (expo / totals).astype(jnp.bfloat16)
            context = jnp.einsum(
                "hqk,khe->qhe", weights, value_seq, preferred_element_type=jnp.float32
            )
            return (context.astype(jnp.bfloat16), highest[:, :, 0] + jnp.log(totals[:, :, 0]))

        contexts, logsums = lax.map(one_block, jnp.arange(SEQ_LEN // length, dtype=jnp.int32))
        return (contexts.reshape(SEQ_LEN, -1), logsums)

    contexts, logsums = lax.map(one_sequence, (queries, keys, values))
    return (contexts.reshape(packed.shape[0], -1), logsums)


def attention_backward(packed, logsums, d_context, slopes):
    queries, keys, values = split_heads(packed)
    d_parted = d_context.reshape(keys.shape[0], SEQ_LEN, keys.shape[2], HEAD_DIM)
    length = min(512, SEQ_LEN)
    factor = 1.0 / math.sqrt(HEAD_DIM)

    def one_sequence(bundle):
        query_seq, key_seq, value_seq, d_seq, logsum_seq = bundle

        def one_block(carry, number):
            d_keys, d_values = carry
            start = number * length
            query_blk = lax.dynamic_slice_in_dim(query_seq, start, length, 0)
            d_blk = lax.dynamic_slice_in_dim(d_seq, start, length, 0)
            scores = score_block(query_blk, key_seq, start, slopes)
            weights = jnp.exp(scores - logsum_seq[number][:, :, None])
            d_weights = jnp.einsum(
                "qhe,khe->hqk", d_blk, value_seq, preferred_element_type=jnp.float32
            )
            centre = jnp.sum(weights * d_weights, axis=2, keepdims=True)
            d_scores = (weights * (d_weights - centre)).astype(jnp.bfloat16)
            d_query = (
                jnp.einsum("hqk,khe->qhe", d_scores, key_seq, preferred_element_type=jnp.float32)
                * factor
            )
            d_keys = (
                d_keys
                + jnp.einsum(
                    "hqk,qhe->khe", d_scores, query_blk, preferred_element_type=jnp.float32
                )
                * factor
            )
            d_values = d_values + jnp.einsum(
                "hqk,qhe->khe",
                weights.astype(jnp.bfloat16),
                d_blk,
                preferred_element_type=jnp.float32,
            )
            return ((d_keys, d_values), d_query)

        zeroed = jnp.zeros(key_seq.shape, jnp.float32)
        (d_keys, d_values), d_queries = lax.scan(
            one_block, (zeroed, zeroed), jnp.arange(SEQ_LEN // length, dtype=jnp.int32)
        )
        return jnp.stack((d_queries.reshape(key_seq.shape), d_keys, d_values), axis=2)

    grads = lax.map(one_sequence, (queries, keys, values, d_parted, logsums))
    return grads.reshape(packed.shape[0], -1).astype(jnp.bfloat16)


def split_shards(
    tokens,
    ln1_gain,
    ln1_bias,
    qkv_weight,
    qkv_bias,
    out_weight,
    out_bias,
    ln2_gain,
    ln2_bias,
    up_weight,
    up_bias,
    down_weight,
    down_bias,
    cotangent,
):
    qkv_cols, up_cols, down_cols, out_cols = (
        lax.all_gather(qkv_weight, "col", axis=0, tiled=True),
        lax.all_gather(up_weight, "col", axis=0, tiled=True),
        lax.all_gather(down_weight, "col", axis=1, tiled=True),
        lax.all_gather(out_weight, "col", axis=1, tiled=True),
    )
    out_rows, down_rows, up_rows, qkv_rows = (
        lax.all_gather(out_weight, "row", axis=0, tiled=True),
        lax.all_gather(down_weight, "row", axis=0, tiled=True),
        lax.all_gather(up_weight, "row", axis=1, tiled=True),
        lax.all_gather(qkv_weight, "row", axis=1, tiled=True),
    )
    inputs = tokens.astype(jnp.float32)
    gain_one = ln1_gain.astype(jnp.float32)
    gain_two = ln2_gain.astype(jnp.float32)
    normed_one, inverse_one, low_one = norm_forward(inputs, gain_one, ln1_bias.astype(jnp.float32))
    rows_one = gather_rows(low_one)
    packed = (sum_cols(rows_one, qkv_cols, False) + qkv_bias.astype(jnp.float32)).astype(
        jnp.bfloat16
    )
    heads_here = packed.shape[1] // (3 * HEAD_DIM)
    head_ids = lax.axis_index("row") * heads_here + jnp.arange(heads_here, dtype=jnp.int32)
    slopes = jnp.exp2(-8.0 * (head_ids.astype(jnp.float32) + 1.0) / HEADS)
    contexts, logsums = attention_forward(packed, slopes)
    context_rows = gather_cols(contexts, False)
    resid = inputs + sum_rows(context_rows, out_rows, False) + out_bias.astype(jnp.float32)
    normed_two, inverse_two, low_two = norm_forward(resid, gain_two, ln2_bias.astype(jnp.float32))
    rows_two = gather_rows(low_two)
    upper = sum_cols(rows_two, up_cols, False) + up_bias.astype(jnp.float32)
    acts = bloom_gelu(upper).astype(jnp.bfloat16)
    act_rows = gather_cols(acts, False)
    output = resid + sum_rows(act_rows, down_rows, False) + down_bias.astype(jnp.float32)
    grad_rows = gather_rows(cotangent)
    d_acts = sum_cols(grad_rows, down_cols, True)
    gelu_pull = jax.vjp(bloom_gelu, upper)[1]
    d_upper = gelu_pull(d_acts)[0].astype(jnp.bfloat16)
    d_upper_rows = gather_cols(d_upper, True)
    d_norm_two = sum_rows(d_upper_rows, up_rows, True)
    d_resid = cotangent.astype(jnp.float32) + norm_backward(
        d_norm_two, normed_two, inverse_two, gain_two
    )
    d_branch_rows = gather_rows(d_resid.astype(jnp.bfloat16))
    d_contexts = sum_cols(d_branch_rows, out_cols, True).astype(jnp.bfloat16)
    d_packed = attention_backward(packed, logsums, d_contexts, slopes)
    d_packed_rows = gather_cols(d_packed, True)
    d_norm_one = sum_rows(d_packed_rows, qkv_rows, True)
    input_grad = d_resid + norm_backward(d_norm_one, normed_one, inverse_one, gain_one)
    weights = (
        lax.psum(weight_grad(rows_one, d_packed_rows).astype(jnp.bfloat16), "dp").astype(
            jnp.float32
        ),
        lax.psum(
            jnp.sum(d_packed_rows, axis=0, dtype=jnp.float32).astype(jnp.bfloat16), "dp"
        ).astype(jnp.float32),
        lax.psum(weight_grad(context_rows, d_branch_rows).astype(jnp.bfloat16), "dp").astype(
            jnp.float32
        ),
        lax.psum(weight_grad(rows_two, d_upper_rows).astype(jnp.bfloat16), "dp").astype(
            jnp.float32
        ),
        lax.psum(
            jnp.sum(d_upper_rows, axis=0, dtype=jnp.float32).astype(jnp.bfloat16), "dp"
        ).astype(jnp.float32),
        lax.psum(weight_grad(act_rows, grad_rows).astype(jnp.bfloat16), "dp").astype(jnp.float32),
    )
    vectors = lax.psum(
        (
            jnp.sum(d_norm_one * normed_one, axis=0),
            jnp.sum(d_norm_one, axis=0),
            jnp.sum(d_resid, axis=0),
            jnp.sum(d_norm_two * normed_two, axis=0),
            jnp.sum(d_norm_two, axis=0),
            jnp.sum(cotangent, axis=0, dtype=jnp.float32),
        ),
        ("dp", "row"),
    )
    return (
        output,
        input_grad,
        vectors[0],
        vectors[1],
        weights[0],
        weights[1],
        weights[2],
        vectors[2],
        vectors[3],
        vectors[4],
        weights[3],
        weights[4],
        weights[5],
        vectors[5],
    )


BLOCK = 256
NT = (((1,), (1,)), ((), ()))
NN = (((1,), (0,)), ((), ()))
TN = (((0,), (0,)), ((), ()))


def mm(left, right, dims):
    return lax.dot_general(left, right, dims, preferred_element_type=jnp.float32)


def key_bias(slope, bias_ref):
    shape = bias_ref.shape
    bias_ref[...] = lax.broadcasted_iota(jnp.int32, shape, 0).astype(jnp.float32) * slope


def scores_t(keys, queries, bias_ref, keep, start, stop):
    scores = mm(keys[:stop], queries, NT) + bias_ref[:stop]
    last = jnp.where(keep, scores[start:], masked)
    return last if start == 0 else jnp.concatenate((scores[:start], last), axis=0)


def lower_mask():
    rows = lax.broadcasted_iota(jnp.int32, (BLOCK, BLOCK), 0)
    return rows <= lax.broadcasted_iota(jnp.int32, (BLOCK, BLOCK), 1)


def forward_kernel(slope_ref, packed_ref, context_ref, lse_ref, bias_ref):
    pair = pl.program_id(0)
    keep = lower_mask()
    for half in range(2):
        base = 3 * HEAD_DIM * half
        key_bias(slope_ref[2 * pair + half], bias_ref)
        queries = packed_ref[:, base : base + 64] * jnp.bfloat16(0.125)
        keys = packed_ref[:, base + 64 : base + 128]
        values_t = packed_ref[:, base + 128 : base + 192].T
        for start in range(0, SEQ_LEN, BLOCK):
            stop = start + BLOCK
            scores = scores_t(keys, queries[start:stop], bias_ref, keep, start, stop)
            highest = jnp.max(scores, axis=0, keepdims=True)
            expo = jnp.exp(scores - highest)
            total = jnp.sum(expo, axis=0, keepdims=True)
            context = mm(values_t[:, :stop], expo.astype(jnp.bfloat16), NN) / total
            context_ref[start:stop, 64 * half : 64 * half + 64] = context.T.astype(jnp.bfloat16)
            lse_ref[0, half : half + 1, start:stop] = highest + jnp.log(total)


def backward_kernel(
    slope_ref, packed_ref, d_context_ref, lse_ref, d_packed_ref, bias_ref, d_keys_ref, d_values_ref
):
    pair = pl.program_id(0)
    keep = lower_mask()
    for half in range(2):
        base = 3 * HEAD_DIM * half
        key_bias(slope_ref[2 * pair + half], bias_ref)
        queries = packed_ref[:, base : base + 64] * jnp.bfloat16(0.125)
        keys = packed_ref[:, base + 64 : base + 128]
        values = packed_ref[:, base + 128 : base + 192]
        keys_t = keys.T
        d_context = d_context_ref[:, 64 * half : 64 * half + 64]
        for start in range(SEQ_LEN - BLOCK, -1, -BLOCK):
            stop = start + BLOCK
            query_blk = queries[start:stop]
            d_blk = d_context[start:stop]
            scores = scores_t(keys, query_blk, bias_ref, keep, start, stop)
            weights = jnp.exp(scores - lse_ref[0, half : half + 1, start:stop])
            weighted = weights * mm(values[:stop], d_blk, NT)
            centre = jnp.sum(weighted, axis=0, keepdims=True)
            d_scores = (weighted - weights * centre).astype(jnp.bfloat16)
            d_query = mm(keys_t[:, :stop], d_scores, NN) * 0.125
            d_packed_ref[start:stop, base : base + 64] = d_query.T.astype(jnp.bfloat16)
            d_keys = mm(d_scores, query_blk, NN)
            d_values = mm(weights.astype(jnp.bfloat16), d_blk, NN)
            if stop == SEQ_LEN:
                d_keys_ref[...] = d_keys
                d_values_ref[...] = d_values
            else:
                d_keys_ref[:stop] += d_keys
                d_values_ref[:stop] += d_values
        d_packed_ref[:, base + 64 : base + 128] = d_keys_ref[...].astype(jnp.bfloat16)
        d_packed_ref[:, base + 128 : base + 192] = d_values_ref[...].astype(jnp.bfloat16)


def fused_forward(packed, slopes):
    pairs = HEADS // 2
    return pl.pallas_call(
        forward_kernel,
        grid=(pairs,),
        out_shape=(
            jax.ShapeDtypeStruct((SEQ_LEN, D), jnp.bfloat16),
            jax.ShapeDtypeStruct((pairs, 2, SEQ_LEN), jnp.float32),
        ),
        in_specs=[
            pl.BlockSpec(memory_space=pltpu.SMEM),
            pl.BlockSpec((SEQ_LEN, 384), lambda i: (0, i)),
        ],
        out_specs=(
            pl.BlockSpec((SEQ_LEN, 128), lambda i: (0, i)),
            pl.BlockSpec((1, 2, SEQ_LEN), lambda i: (i, 0, 0)),
        ),
        scratch_shapes=[pltpu.VMEM((SEQ_LEN, BLOCK), jnp.float32)],
        compiler_params=pltpu.CompilerParams(vmem_limit_bytes=48 * 1024 * 1024),
        cost_estimate=pl.CostEstimate(
            flops=4 * HEADS * SEQ_LEN * SEQ_LEN * 256,
            bytes_accessed=8 * SEQ_LEN * D,
            transcendentals=HEADS * SEQ_LEN * SEQ_LEN,
        ),
        name="attend",
    )(slopes, packed)


def fused_backward(packed, d_context, logsums, slopes):
    pairs = HEADS // 2
    return pl.pallas_call(
        backward_kernel,
        grid=(pairs,),
        out_shape=jax.ShapeDtypeStruct((SEQ_LEN, 3 * D), jnp.bfloat16),
        in_specs=[
            pl.BlockSpec(memory_space=pltpu.SMEM),
            pl.BlockSpec((SEQ_LEN, 384), lambda i: (0, i)),
            pl.BlockSpec((SEQ_LEN, 128), lambda i: (0, i)),
            pl.BlockSpec((1, 2, SEQ_LEN), lambda i: (i, 0, 0)),
        ],
        out_specs=pl.BlockSpec((SEQ_LEN, 384), lambda i: (0, i)),
        scratch_shapes=[
            pltpu.VMEM((SEQ_LEN, BLOCK), jnp.float32),
            pltpu.VMEM((SEQ_LEN, HEAD_DIM), jnp.float32),
            pltpu.VMEM((SEQ_LEN, HEAD_DIM), jnp.float32),
        ],
        compiler_params=pltpu.CompilerParams(vmem_limit_bytes=48 * 1024 * 1024),
        cost_estimate=pl.CostEstimate(
            flops=10 * HEADS * SEQ_LEN * SEQ_LEN * 256,
            bytes_accessed=14 * SEQ_LEN * D,
            transcendentals=HEADS * SEQ_LEN * SEQ_LEN,
        ),
        name="attend_back",
    )(slopes, packed, d_context, logsums)


def local_norm(rows, gain, shift):
    centred = rows - jnp.mean(rows, axis=1, keepdims=True)
    inverse = lax.rsqrt(jnp.mean(centred * centred, axis=1, keepdims=True) + epsilon)
    normed = centred * inverse
    return (normed, inverse, (normed * gain + shift).astype(jnp.bfloat16))


def local_norm_back(grad_rows, normed, inverse, gain):
    scaled = grad_rows * gain
    first = jnp.mean(scaled, axis=1, keepdims=True)
    second = jnp.mean(scaled * normed, axis=1, keepdims=True)
    return inverse * (scaled - first - normed * second)


def swap(value, axis, bit, size):
    return lax.ppermute(value, axis, [(i, i ^ bit) for i in range(size)])


def part(value, index, size, axis):
    return lax.dynamic_slice_in_dim(value, index * size, size, axis)


def whole_weight(weight, rows_on_col):
    names = ("col", "row") if rows_on_col else ("row", "col")
    blocks = lax.all_gather(weight, names, axis=0, tiled=False)
    first, second = (2, 4) if rows_on_col else (4, 2)
    height, width = weight.shape
    blocks = blocks.reshape(first, second, height, width)
    return blocks.transpose(0, 2, 1, 3).reshape(first * height, second * width)


def join_cols(mine, theirs, col):
    return jnp.where(
        col == 0,
        jnp.concatenate((mine, theirs), axis=1),
        jnp.concatenate((theirs, mine), axis=1),
    )


def take_sequence(rows, col):
    mine = part(rows, col, SEQ_LEN, 0)
    theirs = swap(part(rows, 1 - col, SEQ_LEN, 0), "col", 1, 2)
    return join_cols(mine, theirs, col)


def give_features(rows, col):
    half = D // 2
    mine = part(rows, col, half, 1)
    sent = part(rows, 1 - col, half, 1).astype(jnp.bfloat16)
    theirs = swap(sent, "col", 1, 2).astype(jnp.float32)
    return jnp.where(
        col == 0,
        jnp.concatenate((mine, theirs), axis=0),
        jnp.concatenate((theirs, mine), axis=0),
    )


def halve(total, axis_name, bit, size, index, dim):
    half = total.shape[dim] // 2
    theirs = swap(part(total, 1 - index, half, dim), axis_name, bit, size)
    mine = part(total, index, half, dim)
    return (mine.astype(jnp.float32) + theirs.astype(jnp.float32)).astype(jnp.bfloat16)


def core_columns(values, core):
    size = values.shape[1] // 4
    return jnp.concatenate((part(values, core, size, 1), part(values, 2 + core, size, 1)), axis=1)


def scattered_grad(left, right, split_right, row, col, x_first):
    chip, core = row // 2, row % 2
    if split_right:
        sent = mm(left, core_columns(right, 1 - core), TN).astype(jnp.bfloat16)
        own = mm(left, core_columns(right, core), TN)
    else:
        sent = mm(core_columns(left, 1 - core), right, TN).astype(jnp.bfloat16)
        own = mm(core_columns(left, core), right, TN)
    total = (own + swap(sent, "row", 1, 4).astype(jnp.float32)).astype(jnp.bfloat16)
    row_dim = 1 if split_right else 0
    if x_first:
        total = halve(total, "row", 2, 4, chip, row_dim)
        return halve(total, "col", 1, 2, col, 1 - row_dim)
    total = halve(total, "col", 1, 2, col, 1 - row_dim)
    return halve(total, "row", 2, 4, chip, row_dim)


def whole_shards(
    tokens,
    ln1_gain,
    ln1_bias,
    qkv_weight,
    qkv_bias,
    out_weight,
    out_bias,
    ln2_gain,
    ln2_bias,
    up_weight,
    up_bias,
    down_weight,
    down_bias,
    cotangent,
):
    row, col = lax.axis_index("row"), lax.axis_index("col")
    inputs = take_sequence(tokens, col).astype(jnp.float32)
    qkv_all = whole_weight(qkv_weight, True)
    out_all = whole_weight(out_weight, False)
    up_all = whole_weight(up_weight, True)
    down_all = whole_weight(down_weight, False)
    cot = take_sequence(cotangent, col)
    wide = lax.all_gather(
        jnp.concatenate((ln1_gain, ln1_bias, out_bias, ln2_gain, ln2_bias, down_bias)).reshape(
            6, D // 2
        ),
        "col",
        axis=1,
        tiled=True,
    ).astype(jnp.float32)
    gain_one, shift_one, out_shift, gain_two, shift_two, down_shift = (wide[i] for i in range(6))
    inner = lax.all_gather(jnp.concatenate((qkv_bias, up_bias)), "row", axis=0, tiled=False).astype(
        jnp.float32
    )
    qkv_width = qkv_bias.shape[0]
    qkv_shift = inner[:, :qkv_width].reshape(-1)
    up_shift = inner[:, qkv_width:].reshape(-1)

    normed_one, inverse_one, low_one = local_norm(inputs, gain_one, shift_one)
    packed = (mm(low_one, qkv_all, NN) + qkv_shift).astype(jnp.bfloat16)
    slopes = jnp.exp2(-8.0 * (jnp.arange(HEADS, dtype=jnp.float32) + 1.0) / HEADS)
    contexts, logsums = fused_forward(packed, slopes)
    resid = inputs + mm(contexts, out_all, NN) + out_shift
    normed_two, inverse_two, low_two = local_norm(resid, gain_two, shift_two)
    upper = mm(low_two, up_all, NN) + up_shift
    acts = bloom_gelu(upper).astype(jnp.bfloat16)
    down_part = scattered_grad(acts, cot, False, row, col, True)
    output = give_features(resid + mm(acts, down_all, NN) + down_shift, col)
    d_acts = mm(cot, down_all, NT)
    d_upper = jax.vjp(bloom_gelu, upper)[1](d_acts)[0].astype(jnp.bfloat16)
    up_part = scattered_grad(low_two, d_upper, True, row, col, False)
    d_norm_two = mm(d_upper, up_all, NT)
    cot_wide = cot.astype(jnp.float32)
    d_resid = cot_wide + local_norm_back(d_norm_two, normed_two, inverse_two, gain_two)
    d_branch = d_resid.astype(jnp.bfloat16)
    out_part = scattered_grad(contexts, d_branch, False, row, col, True)
    d_contexts = mm(d_branch, out_all, NT).astype(jnp.bfloat16)
    d_packed = fused_backward(packed, d_contexts, logsums, slopes)
    qkv_part = scattered_grad(low_one, d_packed, True, row, col, False)
    d_norm_one = mm(d_packed, qkv_all, NT)
    input_grad = give_features(
        d_resid + local_norm_back(d_norm_one, normed_one, inverse_one, gain_one), col
    )

    down_grad, up_grad = lax.psum((down_part, up_part), "dp")
    qkv_part, out_part, down_grad, up_grad = lax.optimization_barrier(
        (qkv_part, out_part, down_grad, up_grad)
    )
    qkv_grad, out_grad = lax.psum((qkv_part, out_part), "dp")

    sums = lax.psum(
        jnp.concatenate(
            (
                jnp.sum(d_norm_one * normed_one, axis=0),
                jnp.sum(d_norm_one, axis=0),
                jnp.sum(d_resid, axis=0),
                jnp.sum(d_norm_two * normed_two, axis=0),
                jnp.sum(d_norm_two, axis=0),
                jnp.sum(cot_wide, axis=0),
                jnp.sum(d_packed, axis=0, dtype=jnp.float32),
                jnp.sum(d_upper, axis=0, dtype=jnp.float32),
            )
        ),
        ("dp", "row", "col"),
    )
    vectors = [part(sums[i * D : (i + 1) * D], col, D // 2, 0) for i in range(6)]
    qkv_bias_grad = part(sums[6 * D : 9 * D], row, qkv_width, 0)
    up_bias_grad = part(sums[9 * D :], row, up_bias.shape[0], 0)
    wide_grads = [item.astype(jnp.float32) for item in (qkv_grad, out_grad, up_grad, down_grad)]
    return (
        output,
        input_grad,
        vectors[0],
        vectors[1],
        wide_grads[0],
        qkv_bias_grad,
        wide_grads[1],
        vectors[2],
        vectors[3],
        vectors[4],
        wide_grads[2],
        up_bias_grad,
        wide_grads[3],
        vectors[5],
    )


def whole_or_split(n_row, n_col, *arrays):
    if n_row == 4 and n_col == 2 and arrays[0].shape[0] == n_col * SEQ_LEN:
        return whole_shards(*arrays)
    return split_shards(*arrays)


def solution(mesh):
    body = functools.partial(whole_or_split, mesh.shape['row'], mesh.shape['col'])
    placed = (
        P(("dp", "row"), "col"),
        P("col"),
        P("col"),
        P("col", "row"),
        P("row"),
        P("row", "col"),
        P("col"),
        P("col"),
        P("col"),
        P("col", "row"),
        P("row"),
        P("row", "col"),
        P("col"),
        P(("dp", "row"), "col"),
    )
    return jax.shard_map(
        body,
        mesh=mesh,
        in_specs=placed,
        out_specs=(
            P(("dp", "row"), "col"),
            P(("dp", "row"), "col"),
            P("col"),
            P("col"),
            P("col", "row"),
            P("row"),
            P("row", "col"),
            P("col"),
            P("col"),
            P("col"),
            P("col", "row"),
            P("row"),
            P("row", "col"),
            P("col"),
        ),
        check_vma=False,
    )
```

```python
import functools
import math

import jax
import jax.numpy as jnp
from jax import lax
from jax.experimental import pallas as pl
from jax.experimental.pallas import tpu as pltpu
from jax.sharding import PartitionSpec as P

D = 1024
HEADS = 16
HEAD_DIM = 64
SEQ_LEN = 1024


epsilon = 1e-05
masked = -1e30


def bloom_gelu(values):
    return 0.5 * values * (1.0 + jnp.tanh(0.79788456 * values * (1.0 + 0.044715 * values * values)))


def norm_forward(rows, gain, shift):
    middle = lax.psum(jnp.sum(rows, axis=1), "col") / D
    centred = rows - middle[:, None]
    spread = lax.psum(jnp.sum(centred * centred, axis=1), "col") / D
    inverse = lax.rsqrt(spread + epsilon)
    normed = centred * inverse[:, None]
    return (normed, inverse, (normed * gain + shift).astype(jnp.bfloat16))


def norm_backward(grad_rows, normed, inverse, gain):
    scaled = grad_rows * gain
    first, second = lax.psum((jnp.sum(scaled, axis=1), jnp.sum(scaled * normed, axis=1)), "col")
    return inverse[:, None] * (scaled - first[:, None] / D - normed * (second[:, None] / D))


def gather_rows(values):
    return lax.all_gather(values, "row", axis=0, tiled=True)


def gather_cols(values, backward):
    if backward:
        return lax.all_gather(values, "col", axis=0, tiled=True)
    return lax.all_gather(values, "col", axis=0, tiled=True)


def contract_whole(left, right, backward):
    contract = 1 if backward else 0
    return lax.dot_general(
        left, right, (((1,), (contract,)), ((), ())), preferred_element_type=jnp.float32
    )


def sum_cols(left, wide_right, backward):
    swapped = lax.all_to_all(left, "col", split_axis=0, concat_axis=1, tiled=True)
    return contract_whole(swapped, wide_right, backward)


def sum_rows(left, wide_right, backward):
    swapped = lax.all_to_all(left, "row", split_axis=0, concat_axis=1, tiled=True)
    return contract_whole(swapped, wide_right, backward)


def weight_grad(left, grad):
    return lax.dot_general(left, grad, (((0,), (0,)), ((), ())), preferred_element_type=jnp.float32)


def score_block(query_blk, keys, start, slopes):
    scores = jnp.einsum("qhe,khe->hqk", query_blk, keys, preferred_element_type=jnp.float32) * (
        1.0 / math.sqrt(HEAD_DIM)
    )
    shape = (query_blk.shape[0], keys.shape[0])
    offset = (
        lax.broadcasted_iota(jnp.int32, shape, 1)
        - lax.broadcasted_iota(jnp.int32, shape, 0)
        - start
    )
    scores = scores + slopes[:, None, None] * offset.astype(jnp.float32)[None]
    return jnp.where(offset[None] <= 0, scores, masked)


def split_heads(packed):
    heads_here = packed.shape[1] // (3 * HEAD_DIM)
    parted = packed.reshape(packed.shape[0] // SEQ_LEN, SEQ_LEN, heads_here, 3, HEAD_DIM)
    return (parted[:, :, :, 0], parted[:, :, :, 1], parted[:, :, :, 2])


def attention_forward(packed, slopes):
    queries, keys, values = split_heads(packed)
    length = min(512, SEQ_LEN)

    def one_sequence(triple):
        query_seq, key_seq, value_seq = triple

        def one_block(number):
            start = number * length
            query_blk = lax.dynamic_slice_in_dim(query_seq, start, length, 0)
            scores = score_block(query_blk, key_seq, start, slopes)
            highest = jnp.max(scores, axis=2, keepdims=True)
            expo = jnp.exp(scores - highest)
            totals = jnp.sum(expo, axis=2, keepdims=True)
            weights = (expo / totals).astype(jnp.bfloat16)
            context = jnp.einsum(
                "hqk,khe->qhe", weights, value_seq, preferred_element_type=jnp.float32
            )
            return (context.astype(jnp.bfloat16), highest[:, :, 0] + jnp.log(totals[:, :, 0]))

        contexts, logsums = lax.map(one_block, jnp.arange(SEQ_LEN // length, dtype=jnp.int32))
        return (contexts.reshape(SEQ_LEN, -1), logsums)

    contexts, logsums = lax.map(one_sequence, (queries, keys, values))
    return (contexts.reshape(packed.shape[0], -1), logsums)


def attention_backward(packed, logsums, d_context, slopes):
    queries, keys, values = split_heads(packed)
    d_parted = d_context.reshape(keys.shape[0], SEQ_LEN, keys.shape[2], HEAD_DIM)
    length = min(512, SEQ_LEN)
    factor = 1.0 / math.sqrt(HEAD_DIM)

    def one_sequence(bundle):
        query_seq, key_seq, value_seq, d_seq, logsum_seq = bundle

        def one_block(carry, number):
            d_keys, d_values = carry
            start = number * length
            query_blk = lax.dynamic_slice_in_dim(query_seq, start, length, 0)
            d_blk = lax.dynamic_slice_in_dim(d_seq, start, length, 0)
            scores = score_block(query_blk, key_seq, start, slopes)
            weights = jnp.exp(scores - logsum_seq[number][:, :, None])
            d_weights = jnp.einsum(
                "qhe,khe->hqk", d_blk, value_seq, preferred_element_type=jnp.float32
            )
            centre = jnp.sum(weights * d_weights, axis=2, keepdims=True)
            d_scores = (weights * (d_weights - centre)).astype(jnp.bfloat16)
            d_query = (
                jnp.einsum("hqk,khe->qhe", d_scores, key_seq, preferred_element_type=jnp.float32)
                * factor
            )
            d_keys = (
                d_keys
                + jnp.einsum(
                    "hqk,qhe->khe", d_scores, query_blk, preferred_element_type=jnp.float32
                )
                * factor
            )
            d_values = d_values + jnp.einsum(
                "hqk,qhe->khe",
                weights.astype(jnp.bfloat16),
                d_blk,
                preferred_element_type=jnp.float32,
            )
            return ((d_keys, d_values), d_query)

        zeroed = jnp.zeros(key_seq.shape, jnp.float32)
        (d_keys, d_values), d_queries = lax.scan(
            one_block, (zeroed, zeroed), jnp.arange(SEQ_LEN // length, dtype=jnp.int32)
        )
        return jnp.stack((d_queries.reshape(key_seq.shape), d_keys, d_values), axis=2)

    grads = lax.map(one_sequence, (queries, keys, values, d_parted, logsums))
    return grads.reshape(packed.shape[0], -1).astype(jnp.bfloat16)


def split_shards(
    tokens,
    ln1_gain,
    ln1_bias,
    qkv_weight,
    qkv_bias,
    out_weight,
    out_bias,
    ln2_gain,
    ln2_bias,
    up_weight,
    up_bias,
    down_weight,
    down_bias,
    cotangent,
):
    qkv_cols, up_cols, down_cols, out_cols = (
        lax.all_gather(qkv_weight, "col", axis=0, tiled=True),
        lax.all_gather(up_weight, "col", axis=0, tiled=True),
        lax.all_gather(down_weight, "col", axis=1, tiled=True),
        lax.all_gather(out_weight, "col", axis=1, tiled=True),
    )
    out_rows, down_rows, up_rows, qkv_rows = (
        lax.all_gather(out_weight, "row", axis=0, tiled=True),
        lax.all_gather(down_weight, "row", axis=0, tiled=True),
        lax.all_gather(up_weight, "row", axis=1, tiled=True),
        lax.all_gather(qkv_weight, "row", axis=1, tiled=True),
    )
    inputs = tokens.astype(jnp.float32)
    gain_one = ln1_gain.astype(jnp.float32)
    gain_two = ln2_gain.astype(jnp.float32)
    normed_one, inverse_one, low_one = norm_forward(inputs, gain_one, ln1_bias.astype(jnp.float32))
    rows_one = gather_rows(low_one)
    packed = (sum_cols(rows_one, qkv_cols, False) + qkv_bias.astype(jnp.float32)).astype(
        jnp.bfloat16
    )
    heads_here = packed.shape[1] // (3 * HEAD_DIM)
    head_ids = lax.axis_index("row") * heads_here + jnp.arange(heads_here, dtype=jnp.int32)
    slopes = jnp.exp2(-8.0 * (head_ids.astype(jnp.float32) + 1.0) / HEADS)
    contexts, logsums = attention_forward(packed, slopes)
    context_rows = gather_cols(contexts, False)
    resid = inputs + sum_rows(context_rows, out_rows, False) + out_bias.astype(jnp.float32)
    normed_two, inverse_two, low_two = norm_forward(resid, gain_two, ln2_bias.astype(jnp.float32))
    rows_two = gather_rows(low_two)
    upper = sum_cols(rows_two, up_cols, False) + up_bias.astype(jnp.float32)
    acts = bloom_gelu(upper).astype(jnp.bfloat16)
    act_rows = gather_cols(acts, False)
    output = resid + sum_rows(act_rows, down_rows, False) + down_bias.astype(jnp.float32)
    grad_rows = gather_rows(cotangent)
    d_acts = sum_cols(grad_rows, down_cols, True)
    gelu_pull = jax.vjp(bloom_gelu, upper)[1]
    d_upper = gelu_pull(d_acts)[0].astype(jnp.bfloat16)
    d_upper_rows = gather_cols(d_upper, True)
    d_norm_two = sum_rows(d_upper_rows, up_rows, True)
    d_resid = cotangent.astype(jnp.float32) + norm_backward(
        d_norm_two, normed_two, inverse_two, gain_two
    )
    d_branch_rows = gather_rows(d_resid.astype(jnp.bfloat16))
    d_contexts = sum_cols(d_branch_rows, out_cols, True).astype(jnp.bfloat16)
    d_packed = attention_backward(packed, logsums, d_contexts, slopes)
    d_packed_rows = gather_cols(d_packed, True)
    d_norm_one = sum_rows(d_packed_rows, qkv_rows, True)
    input_grad = d_resid + norm_backward(d_norm_one, normed_one, inverse_one, gain_one)
    weights = (
        lax.psum(weight_grad(rows_one, d_packed_rows).astype(jnp.bfloat16), "dp").astype(
            jnp.float32
        ),
        lax.psum(
            jnp.sum(d_packed_rows, axis=0, dtype=jnp.float32).astype(jnp.bfloat16), "dp"
        ).astype(jnp.float32),
        lax.psum(weight_grad(context_rows, d_branch_rows).astype(jnp.bfloat16), "dp").astype(
            jnp.float32
        ),
        lax.psum(weight_grad(rows_two, d_upper_rows).astype(jnp.bfloat16), "dp").astype(
            jnp.float32
        ),
        lax.psum(
            jnp.sum(d_upper_rows, axis=0, dtype=jnp.float32).astype(jnp.bfloat16), "dp"
        ).astype(jnp.float32),
        lax.psum(weight_grad(act_rows, grad_rows).astype(jnp.bfloat16), "dp").astype(jnp.float32),
    )
    vectors = lax.psum(
        (
            jnp.sum(d_norm_one * normed_one, axis=0),
            jnp.sum(d_norm_one, axis=0),
            jnp.sum(d_resid, axis=0),
            jnp.sum(d_norm_two * normed_two, axis=0),
            jnp.sum(d_norm_two, axis=0),
            jnp.sum(cotangent, axis=0, dtype=jnp.float32),
        ),
        ("dp", "row"),
    )
    return (
        output,
        input_grad,
        vectors[0],
        vectors[1],
        weights[0],
        weights[1],
        weights[2],
        vectors[2],
        vectors[3],
        vectors[4],
        weights[3],
        weights[4],
        weights[5],
        vectors[5],
    )


BLOCK = 256
NT = (((1,), (1,)), ((), ()))
NN = (((1,), (0,)), ((), ()))
TN = (((0,), (0,)), ((), ()))


def mm(left, right, dims):
    return lax.dot_general(left, right, dims, preferred_element_type=jnp.float32)


def key_bias(slope, bias_ref):
    shape = bias_ref.shape
    bias_ref[...] = lax.broadcasted_iota(jnp.int32, shape, 0).astype(jnp.float32) * slope


def scores_t(keys, queries, bias_ref, keep, start, stop):
    scores = mm(keys[:stop], queries, NT) + bias_ref[:stop]
    last = jnp.where(keep, scores[start:], masked)
    return last if start == 0 else jnp.concatenate((scores[:start], last), axis=0)


def lower_mask():
    rows = lax.broadcasted_iota(jnp.int32, (BLOCK, BLOCK), 0)
    return rows <= lax.broadcasted_iota(jnp.int32, (BLOCK, BLOCK), 1)


def forward_kernel(slope_ref, packed_ref, context_ref, lse_ref, bias_ref):
    pair = pl.program_id(0)
    keep = lower_mask()
    for half in range(2):
        base = 3 * HEAD_DIM * half
        key_bias(slope_ref[2 * pair + half], bias_ref)
        queries = packed_ref[:, base : base + 64] * jnp.bfloat16(0.125)
        keys = packed_ref[:, base + 64 : base + 128]
        values_t = packed_ref[:, base + 128 : base + 192].T
        for start in range(0, SEQ_LEN, BLOCK):
            stop = start + BLOCK
            scores = scores_t(keys, queries[start:stop], bias_ref, keep, start, stop)
            highest = jnp.max(scores, axis=0, keepdims=True)
            expo = jnp.exp(scores - highest)
            total = jnp.sum(expo, axis=0, keepdims=True)
            context = mm(values_t[:, :stop], expo.astype(jnp.bfloat16), NN) / total
            context_ref[start:stop, 64 * half : 64 * half + 64] = context.T.astype(jnp.bfloat16)
            lse_ref[0, half : half + 1, start:stop] = highest + jnp.log(total)


def backward_kernel(
    slope_ref, packed_ref, d_context_ref, lse_ref, d_packed_ref, bias_ref, d_keys_ref, d_values_ref
):
    pair = pl.program_id(0)
    keep = lower_mask()
    for half in range(2):
        base = 3 * HEAD_DIM * half
        key_bias(slope_ref[2 * pair + half], bias_ref)
        queries = packed_ref[:, base : base + 64] * jnp.bfloat16(0.125)
        keys = packed_ref[:, base + 64 : base + 128]
        values = packed_ref[:, base + 128 : base + 192]
        keys_t = keys.T
        d_context = d_context_ref[:, 64 * half : 64 * half + 64]
        for start in range(SEQ_LEN - BLOCK, -1, -BLOCK):
            stop = start + BLOCK
            query_blk = queries[start:stop]
            d_blk = d_context[start:stop]
            scores = scores_t(keys, query_blk, bias_ref, keep, start, stop)
            weights = jnp.exp(scores - lse_ref[0, half : half + 1, start:stop])
            weighted = weights * mm(values[:stop], d_blk, NT)
            centre = jnp.sum(weighted, axis=0, keepdims=True)
            d_scores = (weighted - weights * centre).astype(jnp.bfloat16)
            d_query = mm(keys_t[:, :stop], d_scores, NN) * 0.125
            d_packed_ref[start:stop, base : base + 64] = d_query.T.astype(jnp.bfloat16)
            d_keys = mm(d_scores, query_blk, NN)
            d_values = mm(weights.astype(jnp.bfloat16), d_blk, NN)
            if stop == SEQ_LEN:
                d_keys_ref[...] = d_keys
                d_values_ref[...] = d_values
            else:
                d_keys_ref[:stop] += d_keys
                d_values_ref[:stop] += d_values
        d_packed_ref[:, base + 64 : base + 128] = d_keys_ref[...].astype(jnp.bfloat16)
        d_packed_ref[:, base + 128 : base + 192] = d_values_ref[...].astype(jnp.bfloat16)


def fused_forward(packed, slopes):
    pairs = HEADS // 2
    return pl.pallas_call(
        forward_kernel,
        grid=(pairs,),
        out_shape=(
            jax.ShapeDtypeStruct((SEQ_LEN, D), jnp.bfloat16),
            jax.ShapeDtypeStruct((pairs, 2, SEQ_LEN), jnp.float32),
        ),
        in_specs=[
            pl.BlockSpec(memory_space=pltpu.SMEM),
            pl.BlockSpec((SEQ_LEN, 384), lambda i: (0, i)),
        ],
        out_specs=(
            pl.BlockSpec((SEQ_LEN, 128), lambda i: (0, i)),
            pl.BlockSpec((1, 2, SEQ_LEN), lambda i: (i, 0, 0)),
        ),
        scratch_shapes=[pltpu.VMEM((SEQ_LEN, BLOCK), jnp.float32)],
        compiler_params=pltpu.CompilerParams(vmem_limit_bytes=48 * 1024 * 1024),
        cost_estimate=pl.CostEstimate(
            flops=4 * HEADS * SEQ_LEN * SEQ_LEN * 256,
            bytes_accessed=8 * SEQ_LEN * D,
            transcendentals=HEADS * SEQ_LEN * SEQ_LEN,
        ),
        name="attend",
    )(slopes, packed)


def fused_backward(packed, d_context, logsums, slopes):
    pairs = HEADS // 2
    return pl.pallas_call(
        backward_kernel,
        grid=(pairs,),
        out_shape=jax.ShapeDtypeStruct((SEQ_LEN, 3 * D), jnp.bfloat16),
        in_specs=[
            pl.BlockSpec(memory_space=pltpu.SMEM),
            pl.BlockSpec((SEQ_LEN, 384), lambda i: (0, i)),
            pl.BlockSpec((SEQ_LEN, 128), lambda i: (0, i)),
            pl.BlockSpec((1, 2, SEQ_LEN), lambda i: (i, 0, 0)),
        ],
        out_specs=pl.BlockSpec((SEQ_LEN, 384), lambda i: (0, i)),
        scratch_shapes=[
            pltpu.VMEM((SEQ_LEN, BLOCK), jnp.float32),
            pltpu.VMEM((SEQ_LEN, HEAD_DIM), jnp.float32),
            pltpu.VMEM((SEQ_LEN, HEAD_DIM), jnp.float32),
        ],
        compiler_params=pltpu.CompilerParams(vmem_limit_bytes=48 * 1024 * 1024),
        cost_estimate=pl.CostEstimate(
            flops=10 * HEADS * SEQ_LEN * SEQ_LEN * 256,
            bytes_accessed=14 * SEQ_LEN * D,
            transcendentals=HEADS * SEQ_LEN * SEQ_LEN,
        ),
        name="attend_back",
    )(slopes, packed, d_context, logsums)


def local_norm(rows, gain, shift):
    centred = rows - jnp.mean(rows, axis=1, keepdims=True)
    inverse = lax.rsqrt(jnp.mean(centred * centred, axis=1, keepdims=True) + epsilon)
    normed = centred * inverse
    return (normed, inverse, (normed * gain + shift).astype(jnp.bfloat16))


def local_norm_back(grad_rows, normed, inverse, gain):
    scaled = grad_rows * gain
    first = jnp.mean(scaled, axis=1, keepdims=True)
    second = jnp.mean(scaled * normed, axis=1, keepdims=True)
    return inverse * (scaled - first - normed * second)


def swap(value, axis, bit, size):
    return lax.ppermute(value, axis, [(i, i ^ bit) for i in range(size)])


def part(value, index, size, axis):
    return lax.dynamic_slice_in_dim(value, index * size, size, axis)


def whole_weight(weight, rows_on_col):
    names, bands = (("row", "col"), 4) if rows_on_col else (("col", "row"), 2)
    blocks = lax.all_gather(weight, names, axis=0, tiled=True)
    height = blocks.shape[0] // bands
    return jnp.concatenate([blocks[i * height : (i + 1) * height] for i in range(bands)], axis=1)


def whole_qkv(weight, wide, inner):
    height, width = weight.shape
    small = jnp.concatenate((wide, inner))
    rows = -(-small.shape[0] // (16 * width)) * 16
    small = jnp.pad(small, (0, rows * width - small.shape[0])).reshape(rows, width)
    blocks = lax.all_gather(
        jnp.concatenate((weight, small), axis=0), ("row", "col"), axis=0, tiled=False
    ).reshape(4, 2, height + rows, width)
    whole = jnp.concatenate(
        [
            jnp.concatenate([blocks[r, c, :height] for c in range(2)], axis=0)
            for r in range(4)
        ],
        axis=1,
    )
    tails = blocks[:, :, height:].reshape(4, 2, -1).astype(jnp.float32)
    size = wide.shape[0]
    wides = tails[0, :, :size].reshape(2, 6, -1).transpose(1, 0, 2).reshape(6, -1)
    return (whole, wides, tails[:, 0, size : size + inner.shape[0]])


def sum_everywhere(vector, n_dp):
    for axis, size, bits in (("row", 4, (1, 2)), ("col", 2, (1,)), ("dp", n_dp, (1, 2))):
        for bit in bits:
            vector = vector + swap(vector, axis, bit, size)
    return vector


def join_cols(mine, theirs, col):
    return jnp.where(
        col == 0,
        jnp.concatenate((mine, theirs), axis=1),
        jnp.concatenate((theirs, mine), axis=1),
    )


def take_sequence(rows, col):
    mine = part(rows, col, SEQ_LEN, 0)
    theirs = swap(part(rows, 1 - col, SEQ_LEN, 0), "col", 1, 2)
    return join_cols(mine, theirs, col)


def give_features(rows, col):
    half = D // 2
    mine = part(rows, col, half, 1)
    sent = part(rows, 1 - col, half, 1).astype(jnp.bfloat16)
    theirs = swap(sent, "col", 1, 2).astype(jnp.float32)
    return jnp.where(
        col == 0,
        jnp.concatenate((mine, theirs), axis=0),
        jnp.concatenate((theirs, mine), axis=0),
    )


def halve(total, axis_name, bit, size, index, dim):
    half = total.shape[dim] // 2
    theirs = swap(part(total, 1 - index, half, dim), axis_name, bit, size)
    mine = part(total, index, half, dim)
    return (mine.astype(jnp.float32) + theirs.astype(jnp.float32)).astype(jnp.bfloat16)


def core_columns(values, core):
    size = values.shape[1] // 4
    return jnp.concatenate((part(values, core, size, 1), part(values, 2 + core, size, 1)), axis=1)


def scattered_grad(left, right, split_right, row, col, x_first):
    chip, core = row // 2, row % 2
    if split_right:
        sent = mm(left, core_columns(right, 1 - core), TN).astype(jnp.bfloat16)
        own = mm(left, core_columns(right, core), TN)
    else:
        sent = mm(core_columns(left, 1 - core), right, TN).astype(jnp.bfloat16)
        own = mm(core_columns(left, core), right, TN)
    total = (own + swap(sent, "row", 1, 4).astype(jnp.float32)).astype(jnp.bfloat16)
    row_dim = 1 if split_right else 0
    if x_first:
        total = halve(total, "row", 2, 4, chip, row_dim)
        return halve(total, "col", 1, 2, col, 1 - row_dim)
    total = halve(total, "col", 1, 2, col, 1 - row_dim)
    return halve(total, "row", 2, 4, chip, row_dim)


def whole_shards(
    n_dp,
    tokens,
    ln1_gain,
    ln1_bias,
    qkv_weight,
    qkv_bias,
    out_weight,
    out_bias,
    ln2_gain,
    ln2_bias,
    up_weight,
    up_bias,
    down_weight,
    down_bias,
    cotangent,
):
    row, col = lax.axis_index("row"), lax.axis_index("col")
    inputs = take_sequence(tokens, col).astype(jnp.float32)
    qkv_all, wide, inner = whole_qkv(
        qkv_weight,
        jnp.concatenate((ln1_gain, ln1_bias, out_bias, ln2_gain, ln2_bias, down_bias)),
        jnp.concatenate((qkv_bias, up_bias)),
    )
    out_all = whole_weight(out_weight, False)
    up_all = whole_weight(up_weight, True)
    down_all = whole_weight(down_weight, False)
    cot = take_sequence(cotangent, col)
    gain_one, shift_one, out_shift, gain_two, shift_two, down_shift = (wide[i] for i in range(6))
    qkv_width = qkv_bias.shape[0]
    qkv_shift = inner[:, :qkv_width].reshape(-1)
    up_shift = inner[:, qkv_width:].reshape(-1)

    normed_one, inverse_one, low_one = local_norm(inputs, gain_one, shift_one)
    packed = (mm(low_one, qkv_all, NN) + qkv_shift).astype(jnp.bfloat16)
    slopes = jnp.exp2(-8.0 * (jnp.arange(HEADS, dtype=jnp.float32) + 1.0) / HEADS)
    contexts, logsums = fused_forward(packed, slopes)
    resid = inputs + mm(contexts, out_all, NN) + out_shift
    normed_two, inverse_two, low_two = local_norm(resid, gain_two, shift_two)
    upper = mm(low_two, up_all, NN) + up_shift
    acts = bloom_gelu(upper).astype(jnp.bfloat16)
    down_part = scattered_grad(acts, cot, False, row, col, True)
    output = give_features(resid + mm(acts, down_all, NN) + down_shift, col)
    d_acts = mm(cot, down_all, NT)
    d_upper = jax.vjp(bloom_gelu, upper)[1](d_acts)[0].astype(jnp.bfloat16)
    up_part = scattered_grad(low_two, d_upper, True, row, col, False)
    d_norm_two = mm(d_upper, up_all, NT)
    cot_wide = cot.astype(jnp.float32)
    d_resid = cot_wide + local_norm_back(d_norm_two, normed_two, inverse_two, gain_two)
    d_branch = d_resid.astype(jnp.bfloat16)
    out_part = scattered_grad(contexts, d_branch, False, row, col, True)
    d_contexts = mm(d_branch, out_all, NT).astype(jnp.bfloat16)
    d_contexts, down_part = lax.optimization_barrier((d_contexts, down_part))
    down_grad = lax.psum(down_part, "dp")
    d_packed = fused_backward(packed, d_contexts, logsums, slopes)
    d_packed, up_part, down_grad = lax.optimization_barrier((d_packed, up_part, down_grad))
    up_grad = lax.psum(up_part, "dp")
    qkv_part = scattered_grad(low_one, d_packed, True, row, col, False)
    d_norm_one = mm(d_packed, qkv_all, NT)
    input_grad = give_features(
        d_resid + local_norm_back(d_norm_one, normed_one, inverse_one, gain_one), col
    )

    qkv_part, out_part, up_grad = lax.optimization_barrier((qkv_part, out_part, up_grad))
    qkv_grad, out_grad = lax.psum((qkv_part, out_part), "dp")

    sums = sum_everywhere(
        jnp.concatenate(
            (
                jnp.sum(d_norm_one * normed_one, axis=0),
                jnp.sum(d_norm_one, axis=0),
                jnp.sum(d_resid, axis=0),
                jnp.sum(d_norm_two * normed_two, axis=0),
                jnp.sum(d_norm_two, axis=0),
                jnp.sum(cot_wide, axis=0),
                jnp.sum(d_packed, axis=0, dtype=jnp.float32),
                jnp.sum(d_upper, axis=0, dtype=jnp.float32),
            )
        ),
        n_dp,
    )
    vectors = [part(sums[i * D : (i + 1) * D], col, D // 2, 0) for i in range(6)]
    qkv_bias_grad = part(sums[6 * D : 9 * D], row, qkv_width, 0)
    up_bias_grad = part(sums[9 * D :], row, up_bias.shape[0], 0)
    wide_grads = [item.astype(jnp.float32) for item in (qkv_grad, out_grad, up_grad, down_grad)]
    return (
        output,
        input_grad,
        vectors[0],
        vectors[1],
        wide_grads[0],
        qkv_bias_grad,
        wide_grads[1],
        vectors[2],
        vectors[3],
        vectors[4],
        wide_grads[2],
        up_bias_grad,
        wide_grads[3],
        vectors[5],
    )


def whole_or_split(n_dp, n_row, n_col, *arrays):
    if n_dp == 4 and n_row == 4 and n_col == 2 and arrays[0].shape[0] == n_col * SEQ_LEN:
        return whole_shards(n_dp, *arrays)
    return split_shards(*arrays)


def solution(mesh):
    body = functools.partial(whole_or_split, *(mesh.shape[name] for name in ('dp', 'row', 'col')))
    placed = (
        P(("dp", "row"), "col"),
        P("col"),
        P("col"),
        P("col", "row"),
        P("row"),
        P("row", "col"),
        P("col"),
        P("col"),
        P("col"),
        P("col", "row"),
        P("row"),
        P("row", "col"),
        P("col"),
        P(("dp", "row"), "col"),
    )
    return jax.shard_map(
        body,
        mesh=mesh,
        in_specs=placed,
        out_specs=(
            P(("dp", "row"), "col"),
            P(("dp", "row"), "col"),
            P("col"),
            P("col"),
            P("col", "row"),
            P("row"),
            P("row", "col"),
            P("col"),
            P("col"),
            P("col"),
            P("col", "row"),
            P("row"),
            P("row", "col"),
            P("col"),
        ),
        check_vma=False,
    )
```
